256 devices in a mesh: param: 4 (over y_lo, core), tile: 64 (over x, y_hi, z).
Axes of the slice: x: 4, y: 4 (y_hi: 2, y_lo: 2; y = y_hi * 2 + y_lo), z: 8, core: 2. Of those that a mesh axis runs over, the one named last changes fastest.
Arguments:
- concentration: float32 [160, 4, 8192], P(None, 'param', 'tile'), may hold values from 0.05 to 3
- reaction_rates: float32 [160, 4, 8192], P(None, None, 'tile'), may hold values from 0.4 to 0.8
- coupling: bfloat16 [160, 160], replicated, may hold values from -0.5 to 0.5
- profile: float32 [16, 160], replicated, may hold values from 0.05 to 0.5
- source_field: float32 [16, 4, 8192], P(None, None, 'tile'), may hold values from 0.1 to 1
- source_map: int32 [64], P('param'), may hold values from 0 to 15
- param_weight: float32 [64], P('param'), may hold values from 0.5 to 2
- sensitivity: bfloat16 [64, 160, 4, 8192], P('param', None, None, 'tile'), may hold values from -6 to 6
- courant: float32 [4, 4, 8192], P(None, None, 'tile'), may hold values from -0.25 to 0.25, as said below
Outputs:
- state_next: float32 [160, 4, 8192], P(None, 'param', 'tile')
- sensitivity_next: bfloat16 [64, 160, 4, 8192], P('param', None, None, 'tile')
The draws below stay inside these ranges and needn't reach their ends.
Inputs may be any that keep to these rules, and one draw needn't show every extreme that they name: `courant`: A cell's east value equals the west value of the next row's cell in the same column, and its north value the south value of the next column's cell in the same row; positive values point toward larger indices.
All inputs are finite; a program needn't handle non-finite values.
Results may differ from the reference program's by a relative error of at most 0.0048.
Values may be sent and summed in bfloat16 or wider, within the bound.
A program may use at most 128 MiB of HBM per device.

```python
import math
from functools import partial
import jax
import jax.numpy as jnp
from jax import lax

S = 160
P_SIZE = 64
NSRC = 16
ITERS = 3
NY = 64
L = 4
NX = 128
CELLS = 8192


def draw_courant(key, part):
    key = jax.random.fold_in(key, 11)
    key_x, key_y = jax.random.split(key, 2)
    faces_x = jax.random.uniform(key_x, (L, NX + 1, NY), jnp.float32, -0.25, 0.25)
    faces_y = jax.random.uniform(key_y, (L, NX, NY + 1), jnp.float32, -0.25, 0.25)
    stacked = jnp.stack([faces_x[:, :NX, :], faces_x[:, 1:, :], faces_y[:, :, :NY], faces_y[:, :, 1:]], axis=0)
    return stacked.reshape(4, L, NX * NY)


def touch_ends(result, key, least, largest):
    index_at = [jax.random.randint(jax.random.fold_in(key, axis), (), 0, length) for axis, length in enumerate(result.shape)]
    widest = result.shape.index(max(result.shape))
    next_to = index_at[:widest] + [(index_at[widest] + 1) % result.shape[widest]] + index_at[widest + 1:]
    return result.at[tuple(index_at)].set(least).at[tuple(next_to)].set(largest)


def steps_of(rng, extent, pieces, smallest, largest):
    def one(axis_at, shards_of):
        steps = jax.random.uniform(jax.random.fold_in(jax.random.fold_in(rng, 6), axis_at), (shards_of,), jnp.float32, smallest / len(pieces), largest / len(pieces))
        return jnp.repeat(jnp.exp(steps), extent[axis_at] // shards_of).reshape((-1,) + (1,) * (len(extent) - axis_at - 1))

    level = one(*pieces[0])
    for cut in pieces[1:]:
        level = level * one(*cut)
    return level


def centred(own_key, extent, width, limit, cuts=(), kind=jnp.bfloat16):
    values = jax.random.normal(own_key, extent, jnp.float32) * width
    if len(cuts) > 0:
        values = steps_of(own_key, extent, cuts, -0.22, 0.18) * values
    return jnp.clip(values, min=-limit, max=limit).astype(kind)


def setup_inputs(seed: int = 0) -> dict:
    seeds = jax.random.split(jax.random.key(seed), 10)
    concentration = jnp.clip(jnp.exp(math.log(3.0) - 4.0943445 * jax.random.uniform(seeds[0], (S, L, CELLS), jnp.float32) ** steps_of(seeds[0], (S, L, CELLS), ((1, 4), (2, 64)), -0.2, 0.2)), 0.05, 3.0)
    reaction_rates = jnp.clip(jnp.exp(math.log(0.8) - 0.6931472 * jax.random.uniform(seeds[1], (S, L, CELLS), jnp.float32) ** steps_of(seeds[1], (S, L, CELLS), ((2, 64),), -0.2, 0.2)), 0.4, 0.8)
    coupling = centred(seeds[2], (S, S), S ** -0.5, 0.5)
    profile = jnp.clip(jnp.exp(jax.random.uniform(seeds[3], (NSRC, S), jnp.float32, math.log(0.05), math.log(0.5))), 0.05, 0.5)
    source_field = jnp.clip(jnp.exp(math.log(1.0) - 2.3025851 * jax.random.uniform(seeds[4], (NSRC, L, CELLS), jnp.float32) ** steps_of(seeds[4], (NSRC, L, CELLS), ((2, 64),), -0.2, 0.2)), 0.1, 1.0)
    source_map = touch_ends(jax.random.randint(seeds[5], (P_SIZE,), 0, NSRC), jax.random.fold_in(seeds[5], 1), 0, NSRC - 1).astype(jnp.int32)
    param_weight = jnp.clip(jnp.exp(math.log(2.0) - 1.3862944 * jax.random.uniform(seeds[6], (P_SIZE,), jnp.float32) ** steps_of(seeds[6], (P_SIZE,), ((0, 4),), -0.2, 0.2)), 0.5, 2.0)
    sensitivity = centred(seeds[7], (P_SIZE, S, L, CELLS), 1.0, 6.0, ((0, 4), (3, 64)))
    courant = draw_courant(jax.random.fold_in(seeds[9], 71), 0)
    return {"concentration": concentration, "reaction_rates": reaction_rates, "coupling": coupling, "profile": profile, "source_field": source_field, "source_map": source_map, "param_weight": param_weight, "sensitivity": sensitivity, "courant": courant}


section_gamma = 1.0 + 1.0 / math.sqrt(2.0)
highest = lax.Precision.HIGHEST

def transport(scalar_field, west_cell, east_cell, courant):
    cell_count = scalar_field.shape[-1]
    column = jnp.arange(cell_count) % NY
    south_cell = jnp.where(column == 0, 0.0, jnp.roll(scalar_field, 1, axis=-1))
    north_cell = jnp.where(column == NY - 1, 0.0, jnp.roll(scalar_field, -1, axis=-1))
    west_face = courant[0]
    east_face = courant[1]
    south_face = courant[2]
    north_face = courant[3]
    inflow_west = jnp.maximum(west_face, 0.0) * west_cell + jnp.minimum(west_face, 0.0) * scalar_field
    outflow_east = jnp.maximum(east_face, 0.0) * scalar_field + jnp.minimum(east_face, 0.0) * east_cell
    inflow_south = jnp.maximum(south_face, 0.0) * south_cell + jnp.minimum(south_face, 0.0) * scalar_field
    outflow_north = jnp.maximum(north_face, 0.0) * scalar_field + jnp.minimum(north_face, 0.0) * north_cell
    return scalar_field + inflow_west - outflow_east + inflow_south - outflow_north

def state_chemistry(start, damping, rate_rows, emission_rows, coupling_float):

    def forcing(state_now):
        return emission_rows + rate_rows * jnp.dot(coupling_float, jnp.tanh(state_now), precision=highest)

    def solve(right_side):
        iterate = right_side
        for sweep in range(ITERS):
            iterate = right_side + section_gamma * rate_rows * jnp.dot(coupling_float, damping * iterate, precision=highest)
        return iterate
    section_one = solve(forcing(start))
    section_two = solve(forcing(start + section_one) - 2.0 * section_one)
    return start + 1.5 * section_one + 0.5 * section_two

def sensitivity_step(advected, source, apply_jacobian):

    def solve(right_side):
        iterate = right_side
        for sweep in range(ITERS):
            iterate = right_side + section_gamma * apply_jacobian(iterate)
        return iterate
    section_one = solve(apply_jacobian(advected) + source)
    section_two = solve(apply_jacobian(advected + section_one) + source - 2.0 * section_one)
    return (advected + 1.5 * section_one + 0.5 * section_two).astype(jnp.bfloat16)

def jacobian_rows(values, damping, reaction_rates, coupling):
    operand = (damping * values).astype(jnp.bfloat16)
    product = jnp.dot(coupling, operand.reshape(operand.shape[0], -1), preferred_element_type=jnp.float32)
    return reaction_rates * product.reshape(values.shape)

def reference(concentration, reaction_rates, coupling, profile, source_field, source_map, param_weight, sensitivity, courant):
    emission = jnp.einsum('ks,klc->slc', profile, source_field, precision=highest)
    zeros_rows = jnp.zeros(concentration.shape[:-1] + (NY,), jnp.float32)
    padded = jnp.concatenate([zeros_rows, concentration, zeros_rows], axis=-1)
    conc_adv = transport(concentration, padded[..., :CELLS], padded[..., 2 * NY:], courant)
    damping = 1.0 - jnp.tanh(conc_adv) ** 2
    species = concentration.shape[0]
    state_next = state_chemistry(conc_adv.reshape(species, -1), damping.reshape(species, -1), reaction_rates.reshape(species, -1), emission.reshape(species, -1), coupling.astype(jnp.float32)).reshape(concentration.shape)
    apply_jacobian = partial(jacobian_rows, damping=damping, reaction_rates=reaction_rates, coupling=coupling)

    def one_param(items):
        values, source_index, weight = items
        base = values.astype(jnp.float32)
        zero_block = jnp.zeros(base.shape[:-1] + (NY,), jnp.float32)
        padded_rows = jnp.concatenate([zero_block, base, zero_block], axis=-1)
        advected = transport(base, padded_rows[..., :CELLS], padded_rows[..., 2 * NY:], courant)
        source = weight * profile[source_index][:, None, None] * source_field[source_index][None]
        return sensitivity_step(advected, source, apply_jacobian)
    sensitivity_next = lax.map(one_param, (sensitivity, source_map, param_weight))
    return (state_next, sensitivity_next)
```

```python
import math
from functools import partial

import jax
import jax.numpy as jnp
from jax import lax
from jax.experimental import pallas as pl
from jax.experimental.pallas import tpu as pltpu
from jax.sharding import PartitionSpec as P

ITERS = 3
NY = 64
LANES = 128
MESH = pl.DeviceIdType.MESH

section_gamma = 1.0 + 1.0 / math.sqrt(2.0)


def series():
    q = [section_gamma**k for k in range(ITERS + 1)]
    square = [0.0] * (2 * ITERS + 2)
    for i, left in enumerate(q):
        for j, right in enumerate(q):
            square[i + j] += left * right
    c = [-value for value in square]
    for k, value in enumerate(q):
        c[k] += 2.0 * value
    for k in range(2 * ITERS + 1):
        c[k + 1] += 0.5 * square[k]
    return c


COEFFS = series()


def rolled(x, shift):
    return pltpu.roll(x, shift, 1)


def face_factors(rows, lane, has_west, has_east):
    west, east, south, north = rows
    column = lane % NY
    first = lane < NY
    plus = [jnp.maximum(face, 0.0) for face in rows]
    minus = [jnp.minimum(face, 0.0) for face in rows]
    own = 1.0 + minus[0] - plus[1] + minus[2] - plus[3]
    from_south = jnp.where(column == 0, 0.0, plus[2])
    from_north = jnp.where(column == NY - 1, 0.0, -minus[3])
    across = jnp.where(first, -minus[1], plus[0])
    halo = jnp.where(first, plus[0] * has_west, -minus[1] * has_east)
    return own, from_south, from_north, across, halo


def inner(q, factors):
    own, from_south, from_north, across, _ = factors
    return (
        own * q
        + from_south * rolled(q, 1)
        + from_north * rolled(q, LANES - 1)
        + across * rolled(q, NY)
    )


def kernel(
    tiles,
    params,
    conc_ref,
    rates_ref,
    coupling_ref,
    profile_ref,
    field_ref,
    courant_ref,
    map_ref,
    weight_ref,
    sens_ref,
    state_ref,
    next_ref,
    sens,
    adv,
    east_out,
    west_out,
    east_in,
    west_in,
    conc_east_out,
    conc_west_out,
    conc_east_in,
    conc_west_in,
    damping,
    rates,
    factors_dw,
    spread,
    work,
    result,
    load_sem,
    store_sem,
    east_send,
    east_recv,
    west_send,
    west_recv,
    conc_send,
    conc_recv,
    damp_send,
    damp_recv,
):
    count, rows, _ = sens.shape
    species, layers = coupling_ref.shape[0], params
    half = rows // 2
    param = lax.axis_index("param")
    tile = lax.axis_index("tile")
    right = lax.rem(tile + 1, tiles)
    left = lax.rem(tile + tiles - 1, tiles)
    has_west = (tile > 0).astype(jnp.float32)
    has_east = (tile < tiles - 1).astype(jnp.float32)
    peers = [(lax.rem(param + k, params), tile) for k in range(1, params)]

    def load(p):
        return pltpu.make_async_copy(sens_ref.at[p], sens.at[p], load_sem.at[p])

    def store(p):
        return pltpu.make_async_copy(result.at[p], next_ref.at[p], store_sem.at[p])

    def remote(src, dst, send, recv, device):
        return pltpu.make_async_remote_copy(
            src_ref=src,
            dst_ref=dst,
            send_sem=send,
            recv_sem=recv,
            device_id=device,
            device_id_type=MESH,
        )

    def send_east(p):
        return remote(
            east_out.at[p], east_in.at[p], east_send.at[p], east_recv.at[p], (param, right)
        )

    def send_west(p):
        return remote(
            west_out.at[p], west_in.at[p], west_send.at[p], west_recv.at[p], (param, left)
        )

    conc_copies = [
        remote(conc_east_out, conc_east_in, conc_send.at[0], conc_recv.at[0], (param, right)),
        remote(conc_west_out, conc_west_in, conc_send.at[1], conc_recv.at[1], (param, left)),
    ]
    damp_copies = [
        remote(
            damping.at[param], damping.at[param], damp_send.at[k], damp_recv.at[k], peers[k]
        )
        for k in range(params - 1)
    ]

    barrier = pltpu.get_barrier_semaphore()
    for device in [(param, right), (param, left)] + peers:
        pl.semaphore_signal(barrier, inc=1, device_id=device, device_id_type=MESH)

    @pl.loop(0, count)
    def _(p):
        load(p).start()

    lane_wide = lax.broadcasted_iota(jnp.int32, (8, LANES), 1)
    lane_one = lax.broadcasted_iota(jnp.int32, (1, LANES), 1)

    def first_lanes(n):
        return lax.broadcasted_iota(jnp.int32, (n, LANES), 1) < NY

    conc = conc_ref[...]
    low, high = conc[: species // 2], conc[species // 2 :]
    turned = rolled(low, NY)
    first = first_lanes(species // 2)
    conc_east_out[...] = jnp.where(first, turned, high)
    conc_west_out[...] = jnp.where(first, high, turned)

    pl.semaphore_wait(barrier, params + 1)
    for copy in conc_copies:
        copy.start()

    faces = [
        jnp.concatenate([courant_ref[pl.ds(layers * f, layers), :]] * (8 // layers), axis=0)
        for f in range(4)
    ]
    wide = face_factors(faces, lane_wide, has_west, has_east)
    wide = [jnp.tile(factor, (rows // 8, 1)) for factor in wide]
    select = first_lanes(half)

    @pl.loop(0, count)
    def _(p):
        load(p).wait()
        q = sens[p].astype(jnp.float32)
        q_low, q_high = q[:half], q[half:]
        across_low = rolled(q_low, NY)
        east_out[p] = jnp.where(select, across_low, q_high).astype(jnp.bfloat16)
        west_out[p] = jnp.where(select, q_high, across_low).astype(jnp.bfloat16)
        send_east(p).start()
        send_west(p).start()
        adv[p] = inner(q, wide)

    own_faces = [courant_ref[pl.ds(layers * f + param, 1), :] for f in range(4)]
    own_factors = face_factors(own_faces, lane_one, has_west, has_east)
    for copy in conc_copies:
        copy.wait_recv()
    east, west = conc_east_in[...], conc_west_in[...]
    conc_halo = jnp.concatenate(
        [jnp.where(first, east, west), rolled(jnp.where(first, west, east), NY)], axis=0
    )
    conc_adv = inner(conc, own_factors) + own_factors[4] * conc_halo
    own_tanh = jnp.tanh(conc_adv)
    own_damping = 1.0 - own_tanh * own_tanh
    damping[param] = own_damping
    for copy in damp_copies:
        copy.start()

    coupling = coupling_ref[...]
    profile = profile_ref[...].T
    own_rates = rates_ref[pl.ds(param, species, stride=layers), :]

    for k in range(profile.shape[1]):
        spread[k] = jnp.broadcast_to(profile[:, k : k + 1], (species, LANES))

    def couple(x):
        top = x.astype(jnp.bfloat16)
        rest = (x - top.astype(jnp.float32)).astype(jnp.bfloat16)
        both = jnp.dot(
            coupling,
            jnp.concatenate([top, rest], axis=1),
            preferred_element_type=jnp.float32,
        )
        return both[:, :LANES] + both[:, LANES:]

    emission = jnp.zeros((species, LANES), jnp.float32)
    for k in range(profile.shape[1]):
        emission += spread[k] * field_ref[pl.ds(layers * k + param, 1), :]

    own_dw = section_gamma * own_rates
    own_scaled = own_dw * own_damping

    def solve(right_side):
        scaled = own_damping * right_side
        z = scaled
        for _ in range(ITERS - 1):
            z = scaled + own_scaled * couple(z)
        return right_side + own_dw * couple(z)

    one = solve(emission + own_rates * couple(own_tanh))
    two = solve(emission + own_rates * couple(jnp.tanh(conc_adv + one)) - 2.0 * one)
    state_ref[...] = conc_adv + 1.5 * one + 0.5 * two

    for copy in damp_copies:
        copy.wait_recv()
    for layer in range(layers):
        rate = rates_ref[pl.ds(layer, species, stride=layers), :]
        here = damping[layer]
        rates[layer] = rate
        product = rate * here
        for k in range(1, 2 * ITERS + 1):
            factors_dw[k, layer] = (COEFFS[k + 1] / COEFFS[k]) * product
        factors_dw[0, layer] = (COEFFS[1] / COEFFS[0]) * rate

    def lanes(parts):
        return jnp.concatenate(parts, axis=1)

    @pl.loop(0, count)
    def _(p):
        east_copy, west_copy = send_east(p), send_west(p)
        east_copy.wait_recv()
        west_copy.wait_recv()
        east, west = east_in[p].astype(jnp.float32), west_in[p].astype(jnp.float32)
        work[:half] = adv[p, :half] + wide[4][:half] * jnp.where(select, east, west)
        work[half:] = adv[p, half:] + wide[4][half:] * rolled(jnp.where(select, west, east), NY)
        source_index = map_ref[p]
        weight = weight_ref[p]
        chosen = spread[source_index]

        a = lanes([work[pl.ds(layer, species, stride=layers), :] for layer in range(layers)])
        field = weight * field_ref[pl.ds(layers * source_index, layers), :]
        source = lanes([chosen * field[layer : layer + 1] for layer in range(layers)])
        d = lanes([damping[layer] for layer in range(layers)])
        w = lanes([rates[layer] for layer in range(layers)])

        def product(z):
            return jnp.dot(coupling, z.astype(jnp.bfloat16), preferred_element_type=jnp.float32)

        v = w * product(d * a) + source
        u = d * v
        z = u
        for k in range(2 * ITERS, 0, -1):
            z = u + lanes([factors_dw[k, layer] for layer in range(layers)]) * product(z)
        out = a + v + lanes([factors_dw[0, layer] for layer in range(layers)]) * product(z)
        for layer in range(layers):
            work[pl.ds(layer, species, stride=layers), :] = out[
                :, layer * LANES : (layer + 1) * LANES
            ]
        result[p] = work[...].astype(jnp.bfloat16)
        store(p).start()

    for copy in conc_copies + damp_copies:
        copy.wait_send()

    @pl.loop(0, count)
    def _(p):
        send_east(p).wait_send()
        send_west(p).wait_send()
        store(p).wait()


def shards(
    concentration,
    reaction_rates,
    coupling,
    profile,
    source_field,
    source_map,
    param_weight,
    sensitivity,
    courant,
):
    tiles, params = lax.axis_size("tile"), lax.axis_size("param")
    species = concentration.shape[0]
    layers = reaction_rates.shape[1]
    count = sensitivity.shape[0]
    sources = profile.shape[0]
    rows = species * layers
    f32, bf16 = jnp.float32, jnp.bfloat16
    vmem = pl.BlockSpec(memory_space=pltpu.VMEM)
    smem = pl.BlockSpec(memory_space=pltpu.SMEM)
    anywhere = pl.BlockSpec(memory_space=pl.ANY)
    halo = pltpu.VMEM((count, rows // 2, LANES), bf16)
    conc_halo = pltpu.VMEM((species // 2, LANES), f32)
    dma = pltpu.SemaphoreType.DMA
    state, following = pl.pallas_call(
        partial(kernel, tiles, params),
        out_shape=(
            jax.ShapeDtypeStruct((species, LANES), f32),
            jax.ShapeDtypeStruct((count, rows, LANES), bf16),
        ),
        in_specs=[vmem] * 6 + [smem] * 2 + [anywhere],
        out_specs=(vmem, anywhere),
        scratch_shapes=[
            pltpu.VMEM((count, rows, LANES), bf16),
            pltpu.VMEM((count, rows, LANES), f32),
            halo,
            halo,
            halo,
            halo,
            conc_halo,
            conc_halo,
            conc_halo,
            conc_halo,
            pltpu.VMEM((layers, species, LANES), f32),
            pltpu.VMEM((layers, species, LANES), f32),
            pltpu.VMEM((2 * ITERS + 1, layers, species, LANES), f32),
            pltpu.VMEM((sources, species, LANES), f32),
            pltpu.VMEM((rows, LANES), f32),
            pltpu.VMEM((count, rows, LANES), bf16),
            dma((count,)),
            dma((count,)),
            dma((count,)),
            dma((count,)),
            dma((count,)),
            dma((count,)),
            dma((2,)),
            dma((2,)),
            dma((params - 1,)),
            dma((params - 1,)),
        ],
        compiler_params=pltpu.CompilerParams(
            collective_id=0, has_side_effects=True, vmem_limit_bytes=56 << 20
        ),
    )(
        concentration.reshape(species, LANES),
        reaction_rates.reshape(rows, LANES),
        coupling,
        profile,
        source_field.reshape(sources * layers, LANES),
        courant.reshape(4 * layers, LANES),
        source_map,
        param_weight,
        sensitivity.reshape(count, rows, LANES),
    )
    return state.reshape(concentration.shape), following.reshape(sensitivity.shape)


def solution(mesh):
    placed = (
        P(None, "param", "tile"),
        P(None, None, "tile"),
        P(),
        P(),
        P(None, None, "tile"),
        P("param"),
        P("param"),
        P("param", None, None, "tile"),
        P(None, None, "tile"),
    )
    return jax.shard_map(
        shards,
        mesh=mesh,
        in_specs=placed,
        out_specs=(P(None, "param", "tile"), P("param", None, None, "tile")),
        check_vma=False,
    )
```

```python
import math
from functools import partial

import jax
import jax.numpy as jnp
from jax import lax
from jax.experimental import pallas as pl
from jax.experimental.pallas import tpu as pltpu
from jax.sharding import PartitionSpec as P

ITERS = 3
NY = 64
LANES = 128
AHEAD = 2
DEPTH = 8
WIRE = jnp.bfloat16
GROUP = 2
MESH = pl.DeviceIdType.MESH

section_gamma = 1.0 + 1.0 / math.sqrt(2.0)


def series():
    q = [section_gamma**k for k in range(ITERS + 1)]
    square = [0.0] * (2 * ITERS + 2)
    for i, left in enumerate(q):
        for j, right in enumerate(q):
            square[i + j] += left * right
    c = [-value for value in square]
    for k, value in enumerate(q):
        c[k] += 2.0 * value
    for k in range(2 * ITERS + 1):
        c[k + 1] += 0.5 * square[k]
    return c


COEFFS = series()


def rolled(x, shift):
    return pltpu.roll(x, shift, 1)


def face_factors(rows, lane, has_west, has_east):
    west, east, south, north = rows
    column = lane % NY
    first = lane < NY
    plus = [jnp.maximum(face, 0.0) for face in rows]
    minus = [jnp.minimum(face, 0.0) for face in rows]
    own = 1.0 + minus[0] - plus[1] + minus[2] - plus[3]
    from_south = jnp.where(column == 0, 0.0, plus[2])
    from_north = jnp.where(column == NY - 1, 0.0, -minus[3])
    across = jnp.where(first, -minus[1], plus[0])
    halo = jnp.where(first, plus[0] * has_west, -minus[1] * has_east)
    return own, from_south, from_north, across, halo


def inner(q, factors):
    own, from_south, from_north, across, _ = factors
    return (
        own * q
        + from_south * rolled(q, 1)
        + from_north * rolled(q, LANES - 1)
        + across * rolled(q, NY)
    )


def kernel(
    tiles,
    params,
    conc_ref,
    rates_ref,
    coupling_ref,
    profile_ref,
    field_ref,
    courant_ref,
    map_ref,
    weight_ref,
    sens_ref,
    state_ref,
    next_ref,
    sens,
    adv,
    east_out,
    west_out,
    east_in,
    west_in,
    relay,
    conc_east_out,
    conc_west_out,
    conc_east_in,
    conc_west_in,
    damping,
    wire,
    rates,
    factors_dw,
    spread,
    work,
    result,
    load_sem,
    store_sem,
    east_send,
    east_recv,
    west_send,
    west_recv,
    conc_send,
    conc_recv,
    damp_send,
    damp_recv,
    relay_send,
    relay_recv,
):
    count, rows, _ = sens.shape
    species, layers = coupling_ref.shape[0], params
    half = rows // 2
    param = lax.axis_index("param")
    tile = lax.axis_index("tile")
    right = lax.rem(tile + 1, tiles)
    left = lax.rem(tile + tiles - 1, tiles)
    has_west = (tile > 0).astype(jnp.float32)
    has_east = (tile < tiles - 1).astype(jnp.float32)
    sibling = param + 1 - 2 * lax.rem(param, 2)
    across = lax.rem(param + 2, params)
    peers = [(sibling, tile), (across, tile)]

    def load(p):
        return pltpu.make_async_copy(sens_ref.at[p], sens.at[p], load_sem.at[p])

    def store(p):
        return pltpu.make_async_copy(result.at[p], next_ref.at[p], store_sem.at[p])

    def remote(src, dst, send, recv, device):
        return pltpu.make_async_remote_copy(
            src_ref=src,
            dst_ref=dst,
            send_sem=send,
            recv_sem=recv,
            device_id=device,
            device_id_type=MESH,
        )

    def send_east(p):
        return remote(
            east_out.at[p], east_in.at[p], east_send.at[p], east_recv.at[p], (param, right)
        )

    def send_west(p):
        return remote(
            west_out.at[p], west_in.at[p], west_send.at[p], west_recv.at[p], (param, left)
        )

    conc_copies = [
        remote(conc_east_out, conc_east_in, conc_send.at[0], conc_recv.at[0], (param, right)),
        remote(conc_west_out, conc_west_in, conc_send.at[1], conc_recv.at[1], (param, left)),
    ]
    damp_copies = [
        remote(wire.at[slot], wire.at[slot], damp_send.at[k], damp_recv.at[k], device)
        for k, (slot, device) in enumerate(
            [(param, (across, tile)), (param, (sibling, tile)), (across, (sibling, tile))]
        )
    ]
    has_left, has_right = tile > 0, tile < tiles - 1
    level = lax.rem(tile, DEPTH)
    top = jnp.logical_and(level == DEPTH - 1, has_right)
    bottom = jnp.logical_and(level == 0, has_left)
    east_direct = jnp.logical_and(level < DEPTH - 1, has_right)
    west_direct = jnp.logical_and(level > 0, has_left)

    def relay_east(p):
        return remote(
            east_out.at[p], relay.at[p], relay_send.at[p], relay_recv.at[p], (across, tile)
        )

    def relay_west(p):
        return remote(
            west_out.at[p], relay.at[p], relay_send.at[p], relay_recv.at[p], (across, tile)
        )

    def onward_east(p):
        return remote(
            relay.at[p], east_in.at[p], east_send.at[p], east_recv.at[p], (across, right)
        )

    def onward_west(p):
        return remote(
            relay.at[p], west_in.at[p], west_send.at[p], west_recv.at[p], (across, left)
        )

    barrier = pltpu.get_barrier_semaphore()
    for device in peers:
        pl.semaphore_signal(barrier, inc=1, device_id=device, device_id_type=MESH)

    @pl.when(has_right)
    def _():
        pl.semaphore_signal(barrier, inc=1, device_id=(param, right), device_id_type=MESH)

    @pl.when(has_left)
    def _():
        pl.semaphore_signal(barrier, inc=1, device_id=(param, left), device_id_type=MESH)

    @pl.when(top)
    def _():
        pl.semaphore_signal(barrier, inc=1, device_id=(across, right), device_id_type=MESH)

    @pl.when(bottom)
    def _():
        pl.semaphore_signal(barrier, inc=1, device_id=(across, left), device_id_type=MESH)

    @pl.when(jnp.logical_not(has_left))
    def _():
        conc_east_in[...] = jnp.zeros_like(conc_east_in)
        east_in[...] = jnp.zeros_like(east_in)

    @pl.when(jnp.logical_not(has_right))
    def _():
        conc_west_in[...] = jnp.zeros_like(conc_west_in)
        west_in[...] = jnp.zeros_like(west_in)

    @pl.loop(0, count)
    def _(p):
        load(p).start()

    lane_wide = lax.broadcasted_iota(jnp.int32, (8, LANES), 1)
    lane_one = lax.broadcasted_iota(jnp.int32, (1, LANES), 1)

    def first_lanes(n):
        return lax.broadcasted_iota(jnp.int32, (n, LANES), 1) < NY

    conc = conc_ref[...]
    low, high = conc[: species // 2], conc[species // 2 :]
    turned = rolled(low, NY)
    first = first_lanes(species // 2)
    conc_east_out[...] = jnp.where(first, turned, high).astype(jnp.bfloat16)
    conc_west_out[...] = jnp.where(first, high, turned).astype(jnp.bfloat16)

    greeted = sum(flag.astype(jnp.int32) for flag in (has_left, has_right, top, bottom))
    pl.semaphore_wait(barrier, len(peers) + greeted)

    pl.when(has_right)(conc_copies[0].start)
    pl.when(has_left)(conc_copies[1].start)

    faces = [
        jnp.concatenate([courant_ref[pl.ds(layers * f, layers), :]] * (8 // layers), axis=0)
        for f in range(4)
    ]
    wide = face_factors(faces, lane_wide, has_west, has_east)
    wide = [jnp.tile(factor, (rows // 8, 1)) for factor in wide]
    select = first_lanes(half)

    def pack(p):
        load(p).wait()
        q = sens[p].astype(jnp.float32)
        q_low, q_high = q[:half], q[half:]
        across_low = rolled(q_low, NY)
        east_out[p] = jnp.where(select, across_low, q_high).astype(jnp.bfloat16)
        west_out[p] = jnp.where(select, q_high, across_low).astype(jnp.bfloat16)
        adv[p] = inner(q, wide)

    def issue(p):
        pl.when(east_direct)(send_east(p).start)
        pl.when(west_direct)(send_west(p).start)
        pl.when(top)(relay_east(p).start)
        pl.when(bottom)(relay_west(p).start)

    def forward(p):
        @pl.when(top)
        def _():
            relay_east(p).wait_recv()
            onward_east(p).start()

        @pl.when(bottom)
        def _():
            relay_west(p).wait_recv()
            onward_west(p).start()

    @pl.loop(0, AHEAD)
    def _(p):
        pack(p)
        issue(p)

    own_faces = [courant_ref[pl.ds(layers * f + param, 1), :] for f in range(4)]
    own_factors = face_factors(own_faces, lane_one, has_west, has_east)
    pl.when(has_left)(conc_copies[0].wait_recv)
    pl.when(has_right)(conc_copies[1].wait_recv)
    east = conc_east_in[...].astype(jnp.float32)
    west = conc_west_in[...].astype(jnp.float32)
    conc_halo = jnp.concatenate(
        [jnp.where(first, east, west), rolled(jnp.where(first, west, east), NY)], axis=0
    )
    conc_adv = inner(conc, own_factors) + own_factors[4] * conc_halo
    own_tanh = jnp.tanh(conc_adv)
    own_damping = 1.0 - own_tanh * own_tanh
    wire[param] = own_damping.astype(WIRE)
    damp_copies[0].start()
    damp_copies[1].start()

    @pl.loop(AHEAD, count)
    def _(p):
        pack(p)
        issue(p)

        @pl.when(p == count // 2)
        def _():
            forward(0)


    damp_copies[0].wait_recv()
    damp_copies[2].start()
    forward(1)

    coupling = coupling_ref[...]
    profile = profile_ref[...].T
    own_rates = rates_ref[pl.ds(param, species, stride=layers), :]

    for k in range(profile.shape[1]):
        spread[k] = jnp.broadcast_to(profile[:, k : k + 1], (species, LANES))

    forwarded = [2]

    def forward_next():
        forward(forwarded[0])
        forwarded[0] += 1

    def couple(x):
        top = x.astype(jnp.bfloat16)
        rest = (x - top.astype(jnp.float32)).astype(jnp.bfloat16)
        both = jnp.dot(
            coupling,
            jnp.concatenate([top, rest], axis=1),
            preferred_element_type=jnp.float32,
        )
        return both[:, :LANES] + both[:, LANES:]

    emission = jnp.zeros((species, LANES), jnp.float32)
    for k in range(profile.shape[1]):
        emission += spread[k] * field_ref[pl.ds(layers * k + param, 1), :]

    own_dw = section_gamma * own_rates
    own_scaled = own_dw * own_damping

    def solve(right_side):
        scaled = own_damping * right_side
        z = scaled
        for _ in range(ITERS - 1):
            z = scaled + own_scaled * couple(z)
        forward_next()
        return right_side + own_dw * couple(z)

    one = solve(emission + own_rates * couple(own_tanh))
    forward_next()
    two = solve(emission + own_rates * couple(jnp.tanh(conc_adv + one)) - 2.0 * one)
    forward_next()
    state_ref[...] = conc_adv + 1.5 * one + 0.5 * two

    for copy in damp_copies[1:]:
        copy.wait_recv()
    for layer in range(layers):
        rate = rates_ref[pl.ds(layer, species, stride=layers), :]
        here = wire[layer].astype(jnp.float32)
        damping[layer] = here
        rates[layer] = rate
        product = rate * here
        for k in range(1, 2 * ITERS + 1):
            factors_dw[k, layer] = (COEFFS[k + 1] / COEFFS[k]) * product
        factors_dw[0, layer] = (COEFFS[1] / COEFFS[0]) * rate

    def lanes(parts):
        return jnp.concatenate(parts, axis=1)

    def gather_edges(p, slot):
        pl.when(has_left)(send_east(p).wait_recv)
        pl.when(has_right)(send_west(p).wait_recv)

        east, west = east_in[p].astype(jnp.float32), west_in[p].astype(jnp.float32)
        here = work.at[slot]
        here[:half] = adv[p, :half] + wide[4][:half] * jnp.where(select, east, west)
        here[half:] = adv[p, half:] + wide[4][half:] * rolled(jnp.where(select, west, east), NY)
        source_index = map_ref[p]
        chosen = spread[source_index]
        field = weight_ref[p] * field_ref[pl.ds(layers * source_index, layers), :]
        a = lanes([here[pl.ds(layer, species, stride=layers), :] for layer in range(layers)])
        source = lanes([chosen * field[layer : layer + 1] for layer in range(layers)])
        return a, source

    def product(z):
        return jnp.dot(coupling, z.astype(jnp.bfloat16), preferred_element_type=jnp.float32)

    @pl.loop(0, count // GROUP)
    def _(group):
        base = group * GROUP
        members = range(GROUP)
        following = forwarded[0] + group + group // 2

        @pl.when(following < count)
        def _():
            forward(following)

        @pl.when(jnp.logical_and(group % 2 == 1, following + 1 < count))
        def _():
            forward(following + 1)

        both = [gather_edges(base + g, g) for g in members]
        d = lanes([damping[layer] for layer in range(layers)])
        w = lanes([rates[layer] for layer in range(layers)])
        v = [w * product(d * a) + source for a, source in both]
        u = [d * value for value in v]
        z = u
        for k in range(2 * ITERS, 0, -1):
            factor = lanes([factors_dw[k, layer] for layer in range(layers)])
            z = [u[g] + factor * product(z[g]) for g in members]
        factor = lanes([factors_dw[0, layer] for layer in range(layers)])
        for g in members:
            out = both[g][0] + v[g] + factor * product(z[g])
            here = work.at[g]
            for layer in range(layers):
                here[pl.ds(layer, species, stride=layers), :] = out[
                    :, layer * LANES : (layer + 1) * LANES
                ]
            result[base + g] = here[...].astype(jnp.bfloat16)
            store(base + g).start()

    for copy in damp_copies:
        copy.wait_send()
    pl.when(has_right)(conc_copies[0].wait_send)
    pl.when(has_left)(conc_copies[1].wait_send)

    @pl.loop(0, count)
    def _(p):
        pl.when(has_right)(send_east(p).wait_send)
        pl.when(has_left)(send_west(p).wait_send)
        pl.when(jnp.logical_or(top, bottom))(relay_east(p).wait_send)
        store(p).wait()


def hand_over(state_from, next_from, state_to, next_to, held, load_sem, store_sem):
    count = next_from.shape[0]

    def load(p):
        return pltpu.make_async_copy(next_from.at[p], held.at[p], load_sem.at[p])

    def store(p):
        return pltpu.make_async_copy(held.at[p], next_to.at[p], store_sem.at[p])

    for p in range(count):
        load(p).start()
    state_to[...] = state_from[...]
    for p in range(count):
        load(p).wait()
        store(p).start()
    for p in range(count):
        store(p).wait()


def shards(
    concentration,
    reaction_rates,
    coupling,
    profile,
    source_field,
    source_map,
    param_weight,
    sensitivity,
    courant,
):
    tiles, params = lax.axis_size("tile"), lax.axis_size("param")
    species = concentration.shape[0]
    layers = reaction_rates.shape[1]
    count = sensitivity.shape[0]
    sources = profile.shape[0]
    rows = species * layers
    f32, bf16 = jnp.float32, jnp.bfloat16
    vmem = pl.BlockSpec(memory_space=pltpu.VMEM)
    smem = pl.BlockSpec(memory_space=pltpu.SMEM)
    anywhere = pl.BlockSpec(memory_space=pl.ANY)
    halo = pltpu.VMEM((count, rows // 2, LANES), bf16)
    conc_halo = pltpu.VMEM((species // 2, LANES), bf16)
    dma = pltpu.SemaphoreType.DMA
    state, following = pl.pallas_call(
        partial(kernel, tiles, params),
        out_shape=(
            jax.ShapeDtypeStruct((species, LANES), f32),
            jax.ShapeDtypeStruct((count, rows, LANES), bf16),
        ),
        in_specs=[vmem] * 6 + [smem] * 2 + [anywhere],
        out_specs=(vmem, anywhere),
        scratch_shapes=[
            pltpu.VMEM((count, rows, LANES), bf16),
            pltpu.VMEM((count, rows, LANES), f32),
            halo,
            halo,
            halo,
            halo,
            halo,
            conc_halo,
            conc_halo,
            conc_halo,
            conc_halo,
            pltpu.VMEM((layers, species, LANES), f32),
            pltpu.VMEM((layers, species, LANES), WIRE),
            pltpu.VMEM((layers, species, LANES), f32),
            pltpu.VMEM((2 * ITERS + 1, layers, species, LANES), f32),
            pltpu.VMEM((sources, species, LANES), f32),
            pltpu.VMEM((GROUP, rows, LANES), f32),
            pltpu.VMEM((count, rows, LANES), bf16),
            dma((count,)),
            dma((count,)),
            dma((count,)),
            dma((count,)),
            dma((count,)),
            dma((count,)),
            dma((2,)),
            dma((2,)),
            dma((3,)),
            dma((3,)),
            dma((count,)),
            dma((count,)),
        ],
        compiler_params=pltpu.CompilerParams(
            collective_id=0, has_side_effects=True, vmem_limit_bytes=60 << 20
        ),
    )(
        concentration.reshape(species, LANES),
        reaction_rates.reshape(rows, LANES),
        coupling,
        profile,
        source_field.reshape(sources * layers, LANES),
        courant.reshape(4 * layers, LANES),
        source_map,
        param_weight,
        sensitivity.reshape(count, rows, LANES),
    )
    state, following = pl.pallas_call(
        hand_over,
        out_shape=(
            jax.ShapeDtypeStruct((species, LANES), f32),
            jax.ShapeDtypeStruct((count, rows, LANES), bf16),
        ),
        in_specs=[vmem, anywhere],
        out_specs=(vmem, anywhere),
        scratch_shapes=[
            pltpu.VMEM((count, rows, LANES), bf16),
            dma((count,)),
            dma((count,)),
        ],
        compiler_params=pltpu.CompilerParams(vmem_limit_bytes=60 << 20),
    )(state, following)
    return state.reshape(concentration.shape), following.reshape(sensitivity.shape)


def solution(mesh):
    placed = (
        P(None, "param", "tile"),
        P(None, None, "tile"),
        P(),
        P(),
        P(None, None, "tile"),
        P("param"),
        P("param"),
        P("param", None, None, "tile"),
        P(None, None, "tile"),
    )
    return jax.shard_map(
        shards,
        mesh=mesh,
        in_specs=placed,
        out_specs=(P(None, "param", "tile"), P("param", None, None, "tile")),
        check_vma=False,
    )
```

```python
import math
from functools import partial

import jax
import jax.numpy as jnp
from jax import lax
from jax.experimental import pallas as pl
from jax.experimental.pallas import tpu as pltpu
from jax.sharding import PartitionSpec as P

ITERS = 3
NY = 64
LANES = 128
STRAIGHT = 2
AHEAD = 2
READY = STRAIGHT + AHEAD
DEPTH = 8
WIRE = jnp.bfloat16
GROUP = 2
MESH = pl.DeviceIdType.MESH

section_gamma = 1.0 + 1.0 / math.sqrt(2.0)


def series():
    q = [section_gamma**k for k in range(ITERS + 1)]
    square = [0.0] * (2 * ITERS + 2)
    for i, left in enumerate(q):
        for j, right in enumerate(q):
            square[i + j] += left * right
    c = [-value for value in square]
    for k, value in enumerate(q):
        c[k] += 2.0 * value
    for k in range(2 * ITERS + 1):
        c[k + 1] += 0.5 * square[k]
    return c


COEFFS = series()


def rolled(x, shift):
    return pltpu.roll(x, shift, 1)


def face_factors(rows, lane, has_west, has_east):
    west, east, south, north = rows
    column = lane % NY
    first = lane < NY
    plus = [jnp.maximum(face, 0.0) for face in rows]
    minus = [jnp.minimum(face, 0.0) for face in rows]
    own = 1.0 + minus[0] - plus[1] + minus[2] - plus[3]
    from_south = jnp.where(column == 0, 0.0, plus[2])
    from_north = jnp.where(column == NY - 1, 0.0, -minus[3])
    across = jnp.where(first, -minus[1], plus[0])
    halo = jnp.where(first, plus[0] * has_west, -minus[1] * has_east)
    return own, from_south, from_north, across, halo


def inner(q, factors):
    own, from_south, from_north, across, _ = factors
    return (
        own * q
        + from_south * rolled(q, 1)
        + from_north * rolled(q, LANES - 1)
        + across * rolled(q, NY)
    )


def kernel(
    tiles,
    params,
    conc_ref,
    rates_ref,
    coupling_ref,
    profile_ref,
    field_ref,
    courant_ref,
    map_ref,
    weight_ref,
    sens_ref,
    state_ref,
    next_ref,
    sens,
    adv,
    east_out,
    west_out,
    east_in,
    west_in,
    relay,
    conc_east_out,
    conc_west_out,
    conc_east_in,
    conc_west_in,
    damping,
    wire,
    rates,
    factors_dw,
    spread,
    work,
    result,
    load_sem,
    store_sem,
    east_send,
    east_recv,
    west_send,
    west_recv,
    conc_send,
    conc_recv,
    damp_send,
    damp_recv,
    relay_send,
    relay_recv,
):
    count, rows, _ = sens.shape
    species, layers = coupling_ref.shape[0], params
    half = rows // 2
    param = lax.axis_index("param")
    tile = lax.axis_index("tile")
    right = lax.rem(tile + 1, tiles)
    left = lax.rem(tile + tiles - 1, tiles)
    has_west = (tile > 0).astype(jnp.float32)
    has_east = (tile < tiles - 1).astype(jnp.float32)
    sibling = param + 1 - 2 * lax.rem(param, 2)
    across = lax.rem(param + 2, params)
    peers = [(sibling, tile), (across, tile)]

    def load(p):
        return pltpu.make_async_copy(sens_ref.at[p], sens.at[p], load_sem.at[p])

    def store(p):
        return pltpu.make_async_copy(result.at[p], next_ref.at[p], store_sem.at[p])

    def remote(src, dst, send, recv, device):
        return pltpu.make_async_remote_copy(
            src_ref=src,
            dst_ref=dst,
            send_sem=send,
            recv_sem=recv,
            device_id=device,
            device_id_type=MESH,
        )

    def send_east(p):
        return remote(
            east_out.at[p], east_in.at[p], east_send.at[p], east_recv.at[p], (param, right)
        )

    def send_west(p):
        return remote(
            west_out.at[p], west_in.at[p], west_send.at[p], west_recv.at[p], (param, left)
        )

    conc_copies = [
        remote(conc_east_out, conc_east_in, conc_send.at[0], conc_recv.at[0], (param, right)),
        remote(conc_west_out, conc_west_in, conc_send.at[1], conc_recv.at[1], (param, left)),
    ]
    damp_copies = [
        remote(wire.at[slot], wire.at[slot], damp_send.at[k], damp_recv.at[k], device)
        for k, (slot, device) in enumerate(
            [(param, (across, tile)), (param, (sibling, tile)), (across, (sibling, tile))]
        )
    ]
    has_left, has_right = tile > 0, tile < tiles - 1
    level = lax.rem(tile, DEPTH)
    top = jnp.logical_and(level == DEPTH - 1, has_right)
    bottom = jnp.logical_and(level == 0, has_left)
    via = jnp.logical_or(top, bottom)
    east_direct = jnp.logical_and(level < DEPTH - 1, has_right)
    west_direct = jnp.logical_and(level > 0, has_left)

    def relay_east(p):
        return remote(
            east_out.at[p], relay.at[p], relay_send.at[p], relay_recv.at[p], (across, tile)
        )

    def relay_west(p):
        return remote(
            west_out.at[p], relay.at[p], relay_send.at[p], relay_recv.at[p], (across, tile)
        )

    def onward_east(p):
        return remote(
            relay.at[p], east_in.at[p], east_send.at[p], east_recv.at[p], (across, right)
        )

    def onward_west(p):
        return remote(
            relay.at[p], west_in.at[p], west_send.at[p], west_recv.at[p], (across, left)
        )

    barrier = pltpu.get_barrier_semaphore()
    for device in peers:
        pl.semaphore_signal(barrier, inc=1, device_id=device, device_id_type=MESH)

    @pl.when(has_right)
    def _():
        pl.semaphore_signal(barrier, inc=1, device_id=(param, right), device_id_type=MESH)

    @pl.when(has_left)
    def _():
        pl.semaphore_signal(barrier, inc=1, device_id=(param, left), device_id_type=MESH)

    @pl.when(top)
    def _():
        pl.semaphore_signal(barrier, inc=1, device_id=(across, right), device_id_type=MESH)

    @pl.when(bottom)
    def _():
        pl.semaphore_signal(barrier, inc=1, device_id=(across, left), device_id_type=MESH)

    @pl.when(jnp.logical_not(has_left))
    def _():
        conc_east_in[...] = jnp.zeros_like(conc_east_in)
        east_in[...] = jnp.zeros_like(east_in)

    @pl.when(jnp.logical_not(has_right))
    def _():
        conc_west_in[...] = jnp.zeros_like(conc_west_in)
        west_in[...] = jnp.zeros_like(west_in)

    @pl.loop(0, count)
    def _(p):
        load(p).start()

    lane_wide = lax.broadcasted_iota(jnp.int32, (8, LANES), 1)
    lane_one = lax.broadcasted_iota(jnp.int32, (1, LANES), 1)

    def first_lanes(n):
        return lax.broadcasted_iota(jnp.int32, (n, LANES), 1) < NY

    conc = conc_ref[...]
    low, high = conc[: species // 2], conc[species // 2 :]
    turned = rolled(low, NY)
    first = first_lanes(species // 2)
    conc_east_out[...] = jnp.where(first, turned, high).astype(jnp.bfloat16)
    conc_west_out[...] = jnp.where(first, high, turned).astype(jnp.bfloat16)

    faces = [
        jnp.concatenate([courant_ref[pl.ds(layers * f, layers), :]] * (8 // layers), axis=0)
        for f in range(4)
    ]
    wide = face_factors(faces, lane_wide, has_west, has_east)
    wide = [jnp.tile(factor, (rows // 8, 1)) for factor in wide]
    select = first_lanes(half)

    def pack(p):
        load(p).wait()
        q = sens[p].astype(jnp.float32)
        q_low, q_high = q[:half], q[half:]
        across_low = rolled(q_low, NY)
        east_out[p] = jnp.where(select, across_low, q_high).astype(jnp.bfloat16)
        west_out[p] = jnp.where(select, q_high, across_low).astype(jnp.bfloat16)
        adv[p] = inner(q, wide)

    pl.loop(0, READY)(pack)

    greeted = sum(flag.astype(jnp.int32) for flag in (has_left, has_right, top, bottom))
    pl.semaphore_wait(barrier, len(peers) + greeted)

    pl.when(has_right)(conc_copies[0].start)
    pl.when(has_left)(conc_copies[1].start)

    def issue(p):
        straight = p < STRAIGHT
        pl.when(jnp.logical_and(top, p >= STRAIGHT))(lambda: relay_east(p).start())
        pl.when(jnp.logical_and(bottom, p >= STRAIGHT))(lambda: relay_west(p).start())
        pl.when(jnp.logical_or(east_direct, jnp.logical_and(top, straight)))(
            lambda: send_east(p).start()
        )
        pl.when(jnp.logical_or(west_direct, jnp.logical_and(bottom, straight)))(
            lambda: send_west(p).start()
        )

    def forward(step):
        p = step + STRAIGHT
        pl.when(jnp.logical_and(via, p + AHEAD < count))(lambda: issue(p + AHEAD))

        @pl.when(jnp.logical_and(top, p < count))
        def _():
            relay_east(p).wait_recv()
            onward_east(p).start()

        @pl.when(jnp.logical_and(bottom, p < count))
        def _():
            relay_west(p).wait_recv()
            onward_west(p).start()

    pl.loop(0, READY)(lambda step: issue(READY - 1 - step))

    @pl.loop(READY, count)
    def _(p):
        pack(p)
        pl.when(jnp.logical_not(via))(lambda: issue(p))

        @pl.when(p == count // 2)
        def _():
            forward(0)

    forward(1)

    own_faces = [courant_ref[pl.ds(layers * f + param, 1), :] for f in range(4)]
    own_factors = face_factors(own_faces, lane_one, has_west, has_east)
    pl.when(has_left)(conc_copies[0].wait_recv)
    pl.when(has_right)(conc_copies[1].wait_recv)
    east = conc_east_in[...].astype(jnp.float32)
    west = conc_west_in[...].astype(jnp.float32)
    conc_halo = jnp.concatenate(
        [jnp.where(first, east, west), rolled(jnp.where(first, west, east), NY)], axis=0
    )
    conc_adv = inner(conc, own_factors) + own_factors[4] * conc_halo
    own_tanh = jnp.tanh(conc_adv)
    own_damping = 1.0 - own_tanh * own_tanh
    wire[param] = own_damping.astype(WIRE)
    damp_copies[0].start()
    damp_copies[1].start()

    forward(2)

    coupling = coupling_ref[...]
    profile = profile_ref[...].T
    own_rates = rates_ref[pl.ds(param, species, stride=layers), :]

    for k in range(profile.shape[1]):
        spread[k] = jnp.broadcast_to(profile[:, k : k + 1], (species, LANES))

    forwarded = [3]

    def forward_next():
        forward(forwarded[0])
        forwarded[0] += 1

    def couple(x):
        top = x.astype(jnp.bfloat16)
        rest = (x - top.astype(jnp.float32)).astype(jnp.bfloat16)
        both = jnp.dot(
            coupling,
            jnp.concatenate([top, rest], axis=1),
            preferred_element_type=jnp.float32,
        )
        return both[:, :LANES] + both[:, LANES:]

    emission = jnp.zeros((species, LANES), jnp.float32)
    for k in range(profile.shape[1]):
        emission += spread[k] * field_ref[pl.ds(layers * k + param, 1), :]

    forward_next()
    damp_copies[0].wait_recv()
    damp_copies[2].start()

    own_dw = section_gamma * own_rates
    own_scaled = own_dw * own_damping

    def solve(right_side):
        scaled = own_damping * right_side
        z = scaled
        for _ in range(ITERS - 1):
            z = scaled + own_scaled * couple(z)
        return right_side + own_dw * couple(z)

    one = solve(emission + own_rates * couple(own_tanh))
    forward_next()
    two = solve(emission + own_rates * couple(jnp.tanh(conc_adv + one)) - 2.0 * one)
    forward_next()
    state_ref[...] = conc_adv + 1.5 * one + 0.5 * two

    for copy in damp_copies[1:]:
        copy.wait_recv()
    for layer in range(layers):
        rate = rates_ref[pl.ds(layer, species, stride=layers), :]
        here = wire[layer].astype(jnp.float32)
        damping[layer] = here
        rates[layer] = rate
        product = rate * here
        for k in range(1, 2 * ITERS + 1):
            factors_dw[k, layer] = (COEFFS[k + 1] / COEFFS[k]) * product
        factors_dw[0, layer] = (COEFFS[1] / COEFFS[0]) * rate

    def lanes(parts):
        return jnp.concatenate(parts, axis=1)

    def gather_edges(p, slot):
        pl.when(has_left)(send_east(p).wait_recv)
        pl.when(has_right)(send_west(p).wait_recv)

        east, west = east_in[p].astype(jnp.float32), west_in[p].astype(jnp.float32)
        here = work.at[slot]
        here[:half] = adv[p, :half] + wide[4][:half] * jnp.where(select, east, west)
        here[half:] = adv[p, half:] + wide[4][half:] * rolled(jnp.where(select, west, east), NY)
        source_index = map_ref[p]
        chosen = spread[source_index]
        field = weight_ref[p] * field_ref[pl.ds(layers * source_index, layers), :]
        a = lanes([here[pl.ds(layer, species, stride=layers), :] for layer in range(layers)])
        source = lanes([chosen * field[layer : layer + 1] for layer in range(layers)])
        return a, source

    def product(z):
        return jnp.dot(coupling, z.astype(jnp.bfloat16), preferred_element_type=jnp.float32)

    @pl.loop(0, count // GROUP)
    def _(group):
        base = group * GROUP
        members = range(GROUP)
        late = count // (2 * GROUP)
        following = forwarded[0] + group + jnp.maximum(group - late, 0)
        forward(following)
        pl.when(group >= late)(lambda: forward(following + 1))

        both = [gather_edges(base + g, g) for g in members]
        d = lanes([damping[layer] for layer in range(layers)])
        w = lanes([rates[layer] for layer in range(layers)])
        v = [w * product(d * a) + source for a, source in both]
        u = [d * value for value in v]
        z = u
        for k in range(2 * ITERS, 0, -1):
            factor = lanes([factors_dw[k, layer] for layer in range(layers)])
            z = [u[g] + factor * product(z[g]) for g in members]
        factor = lanes([factors_dw[0, layer] for layer in range(layers)])
        for g in members:
            out = both[g][0] + v[g] + factor * product(z[g])
            here = work.at[g]
            for layer in range(layers):
                here[pl.ds(layer, species, stride=layers), :] = out[
                    :, layer * LANES : (layer + 1) * LANES
                ]
            result[base + g] = here[...].astype(jnp.bfloat16)
            store(base + g).start()

    for copy in damp_copies:
        copy.wait_send()
    pl.when(has_right)(conc_copies[0].wait_send)
    pl.when(has_left)(conc_copies[1].wait_send)

    @pl.loop(0, count)
    def _(p):
        pl.when(has_right)(send_east(p).wait_send)
        pl.when(has_left)(send_west(p).wait_send)
        pl.when(jnp.logical_and(via, p >= STRAIGHT))(lambda: relay_east(p).wait_send())
        store(p).wait()


def hand_over(state_from, next_from, state_to, next_to, state_held, held, load_sem, store_sem):
    count = next_from.shape[0]

    def pairs(p):
        if p == count:
            return state_from, state_held, state_to
        return next_from.at[p], held.at[p], next_to.at[p]

    def load(p):
        source, here, _ = pairs(p)
        return pltpu.make_async_copy(source, here, load_sem.at[p])

    def store(p):
        _, here, target = pairs(p)
        return pltpu.make_async_copy(here, target, store_sem.at[p])

    for p in range(count + 1):
        load(p).start()
    for p in range(count + 1):
        load(p).wait()
        store(p).start()
    for p in range(count + 1):
        store(p).wait()


def shards(
    concentration,
    reaction_rates,
    coupling,
    profile,
    source_field,
    source_map,
    param_weight,
    sensitivity,
    courant,
):
    tiles, params = lax.axis_size("tile"), lax.axis_size("param")
    species = concentration.shape[0]
    layers = reaction_rates.shape[1]
    count = sensitivity.shape[0]
    sources = profile.shape[0]
    rows = species * layers
    f32, bf16 = jnp.float32, jnp.bfloat16
    vmem = pl.BlockSpec(memory_space=pltpu.VMEM)
    smem = pl.BlockSpec(memory_space=pltpu.SMEM)
    anywhere = pl.BlockSpec(memory_space=pl.ANY)
    halo = pltpu.VMEM((count, rows // 2, LANES), bf16)
    conc_halo = pltpu.VMEM((species // 2, LANES), bf16)
    dma = pltpu.SemaphoreType.DMA
    state, following = pl.pallas_call(
        partial(kernel, tiles, params),
        out_shape=(
            jax.ShapeDtypeStruct((species, LANES), f32),
            jax.ShapeDtypeStruct((count, rows, LANES), bf16),
        ),
        in_specs=[vmem] * 6 + [smem] * 2 + [anywhere],
        out_specs=(vmem, anywhere),
        scratch_shapes=[
            pltpu.VMEM((count, rows, LANES), bf16),
            pltpu.VMEM((count, rows, LANES), f32),
            halo,
            halo,
            halo,
            halo,
            halo,
            conc_halo,
            conc_halo,
            conc_halo,
            conc_halo,
            pltpu.VMEM((layers, species, LANES), f32),
            pltpu.VMEM((layers, species, LANES), WIRE),
            pltpu.VMEM((layers, species, LANES), f32),
            pltpu.VMEM((2 * ITERS + 1, layers, species, LANES), f32),
            pltpu.VMEM((sources, species, LANES), f32),
            pltpu.VMEM((GROUP, rows, LANES), f32),
            pltpu.VMEM((count, rows, LANES), bf16),
            dma((count,)),
            dma((count,)),
            dma((count,)),
            dma((count,)),
            dma((count,)),
            dma((count,)),
            dma((2,)),
            dma((2,)),
            dma((3,)),
            dma((3,)),
            dma((count,)),
            dma((count,)),
        ],
        compiler_params=pltpu.CompilerParams(
            collective_id=0, has_side_effects=True, vmem_limit_bytes=60 << 20
        ),
    )(
        concentration.reshape(species, LANES),
        reaction_rates.reshape(rows, LANES),
        coupling,
        profile,
        source_field.reshape(sources * layers, LANES),
        courant.reshape(4 * layers, LANES),
        source_map,
        param_weight,
        sensitivity.reshape(count, rows, LANES),
    )
    state, following = pl.pallas_call(
        hand_over,
        out_shape=(
            jax.ShapeDtypeStruct((species, LANES), f32),
            jax.ShapeDtypeStruct((count, rows, LANES), bf16),
        ),
        in_specs=[anywhere] * 2,
        out_specs=(anywhere,) * 2,
        scratch_shapes=[
            pltpu.VMEM((species, LANES), f32),
            pltpu.VMEM((count, rows, LANES), bf16),
            dma((count + 1,)),
            dma((count + 1,)),
        ],
        compiler_params=pltpu.CompilerParams(vmem_limit_bytes=60 << 20),
    )(state, following)
    return state.reshape(concentration.shape), following.reshape(sensitivity.shape)


def solution(mesh):
    placed = (
        P(None, "param", "tile"),
        P(None, None, "tile"),
        P(),
        P(),
        P(None, None, "tile"),
        P("param"),
        P("param"),
        P("param", None, None, "tile"),
        P(None, None, "tile"),
    )
    return jax.shard_map(
        shards,
        mesh=mesh,
        in_specs=placed,
        out_specs=(P(None, "param", "tile"), P("param", None, None, "tile")),
        check_vma=False,
    )
```

```python
import math
from functools import partial

import jax
import jax.numpy as jnp
from jax import lax
from jax.experimental import pallas as pl
from jax.experimental.pallas import tpu as pltpu
from jax.sharding import PartitionSpec as P

ITERS = 3
NY = 64
LANES = 128
STRAIGHT = 2
AHEAD = 2
READY = STRAIGHT + AHEAD
DEPTH = 8
WIRE = jnp.bfloat16
GROUP = 2
MESH = pl.DeviceIdType.MESH

section_gamma = 1.0 + 1.0 / math.sqrt(2.0)


def series():
    q = [section_gamma**k for k in range(ITERS + 1)]
    square = [0.0] * (2 * ITERS + 2)
    for i, left in enumerate(q):
        for j, right in enumerate(q):
            square[i + j] += left * right
    c = [-value for value in square]
    for k, value in enumerate(q):
        c[k] += 2.0 * value
    for k in range(2 * ITERS + 1):
        c[k + 1] += 0.5 * square[k]
    return c


COEFFS = series()


def rolled(x, shift):
    return pltpu.roll(x, shift, 1)


def face_factors(rows, lane, has_west, has_east):
    west, east, south, north = rows
    column = lane % NY
    first = lane < NY
    plus = [jnp.maximum(face, 0.0) for face in rows]
    minus = [jnp.minimum(face, 0.0) for face in rows]
    own = 1.0 + minus[0] - plus[1] + minus[2] - plus[3]
    from_south = jnp.where(column == 0, 0.0, plus[2])
    from_north = jnp.where(column == NY - 1, 0.0, -minus[3])
    across = jnp.where(first, -minus[1], plus[0])
    halo = jnp.where(first, plus[0] * has_west, -minus[1] * has_east)
    return own, from_south, from_north, across, halo


def inner(q, factors):
    own, from_south, from_north, across, _ = factors
    return (
        own * q
        + from_south * rolled(q, 1)
        + from_north * rolled(q, LANES - 1)
        + across * rolled(q, NY)
    )


def kernel(
    tiles,
    params,
    conc_ref,
    rates_ref,
    coupling_ref,
    profile_ref,
    field_ref,
    courant_ref,
    map_ref,
    weight_ref,
    sens_ref,
    state_ref,
    next_ref,
    sens,
    adv,
    east_out,
    west_out,
    east_in,
    west_in,
    relay,
    conc_east_out,
    conc_west_out,
    conc_east_in,
    conc_west_in,
    damping,
    wire,
    rates,
    factors_dw,
    spread,
    work,
    result,
    load_sem,
    store_sem,
    east_send,
    east_recv,
    west_send,
    west_recv,
    conc_send,
    conc_recv,
    damp_send,
    damp_recv,
    relay_send,
    relay_recv,
):
    count, rows, _ = sens.shape
    species, layers = coupling_ref.shape[0], params
    half = rows // 2
    param = lax.axis_index("param")
    tile = lax.axis_index("tile")
    right = lax.rem(tile + 1, tiles)
    left = lax.rem(tile + tiles - 1, tiles)
    has_west = (tile > 0).astype(jnp.float32)
    has_east = (tile < tiles - 1).astype(jnp.float32)
    sibling = param + 1 - 2 * lax.rem(param, 2)
    across = lax.rem(param + 2, params)
    peers = [(sibling, tile), (across, tile)]

    def load(p):
        return pltpu.make_async_copy(sens_ref.at[p], sens.at[p], load_sem.at[p])

    def store(p):
        return pltpu.make_async_copy(result.at[p], next_ref.at[p], store_sem.at[p])

    def remote(src, dst, send, recv, device):
        return pltpu.make_async_remote_copy(
            src_ref=src,
            dst_ref=dst,
            send_sem=send,
            recv_sem=recv,
            device_id=device,
            device_id_type=MESH,
        )

    def send_east(p):
        return remote(
            east_out.at[p], east_in.at[p], east_send.at[p], east_recv.at[p], (param, right)
        )

    def send_west(p):
        return remote(
            west_out.at[p], west_in.at[p], west_send.at[p], west_recv.at[p], (param, left)
        )

    conc_copies = [
        remote(conc_east_out, conc_east_in, conc_send.at[0], conc_recv.at[0], (param, right)),
        remote(conc_west_out, conc_west_in, conc_send.at[1], conc_recv.at[1], (param, left)),
    ]
    damp_copies = [
        remote(wire.at[slot], wire.at[slot], damp_send.at[k], damp_recv.at[k], device)
        for k, (slot, device) in enumerate(
            [(param, (across, tile)), (param, (sibling, tile)), (across, (sibling, tile))]
        )
    ]
    has_left, has_right = tile > 0, tile < tiles - 1
    level = lax.rem(tile, DEPTH)
    top = jnp.logical_and(level == DEPTH - 1, has_right)
    bottom = jnp.logical_and(level == 0, has_left)
    via = jnp.logical_or(top, bottom)
    east_direct = jnp.logical_and(level < DEPTH - 1, has_right)
    west_direct = jnp.logical_and(level > 0, has_left)

    def relay_east(p):
        return remote(
            east_out.at[p], relay.at[p], relay_send.at[p], relay_recv.at[p], (across, tile)
        )

    def relay_west(p):
        return remote(
            west_out.at[p], relay.at[p], relay_send.at[p], relay_recv.at[p], (across, tile)
        )

    def onward_east(p):
        return remote(
            relay.at[p], east_in.at[p], east_send.at[p], east_recv.at[p], (across, right)
        )

    def onward_west(p):
        return remote(
            relay.at[p], west_in.at[p], west_send.at[p], west_recv.at[p], (across, left)
        )

    barrier = pltpu.get_barrier_semaphore()
    for device in peers:
        pl.semaphore_signal(barrier, inc=1, device_id=device, device_id_type=MESH)

    @pl.when(has_right)
    def _():
        pl.semaphore_signal(barrier, inc=1, device_id=(param, right), device_id_type=MESH)

    @pl.when(has_left)
    def _():
        pl.semaphore_signal(barrier, inc=1, device_id=(param, left), device_id_type=MESH)

    @pl.when(top)
    def _():
        pl.semaphore_signal(barrier, inc=1, device_id=(across, right), device_id_type=MESH)

    @pl.when(bottom)
    def _():
        pl.semaphore_signal(barrier, inc=1, device_id=(across, left), device_id_type=MESH)

    @pl.when(jnp.logical_not(has_left))
    def _():
        conc_east_in[...] = jnp.zeros_like(conc_east_in)
        east_in[...] = jnp.zeros_like(east_in)

    @pl.when(jnp.logical_not(has_right))
    def _():
        conc_west_in[...] = jnp.zeros_like(conc_west_in)
        west_in[...] = jnp.zeros_like(west_in)

    @pl.loop(0, count)
    def _(p):
        load(p).start()

    lane_wide = lax.broadcasted_iota(jnp.int32, (8, LANES), 1)
    lane_one = lax.broadcasted_iota(jnp.int32, (1, LANES), 1)

    def first_lanes(n):
        return lax.broadcasted_iota(jnp.int32, (n, LANES), 1) < NY

    conc = conc_ref[...]
    low, high = conc[: species // 2], conc[species // 2 :]
    turned = rolled(low, NY)
    first = first_lanes(species // 2)
    conc_east_out[...] = jnp.where(first, turned, high).astype(jnp.bfloat16)
    conc_west_out[...] = jnp.where(first, high, turned).astype(jnp.bfloat16)

    faces = [
        jnp.concatenate([courant_ref[pl.ds(layers * f, layers), :]] * (8 // layers), axis=0)
        for f in range(4)
    ]
    wide = face_factors(faces, lane_wide, has_west, has_east)
    wide = [jnp.tile(factor, (rows // 8, 1)) for factor in wide]
    select = first_lanes(half)

    def pack(p):
        load(p).wait()
        q = sens[p].astype(jnp.float32)
        q_low, q_high = q[:half], q[half:]
        across_low = rolled(q_low, NY)
        east_out[p] = jnp.where(select, across_low, q_high).astype(jnp.bfloat16)
        west_out[p] = jnp.where(select, q_high, across_low).astype(jnp.bfloat16)
        adv[p] = inner(q, wide)

    pl.loop(0, READY)(pack)

    greeted = sum(flag.astype(jnp.int32) for flag in (has_left, has_right, top, bottom))
    pl.semaphore_wait(barrier, len(peers) + greeted)

    pl.when(has_right)(conc_copies[0].start)
    pl.when(has_left)(conc_copies[1].start)

    def issue(p):
        straight = p < STRAIGHT
        pl.when(jnp.logical_and(top, p >= STRAIGHT))(lambda: relay_east(p).start())
        pl.when(jnp.logical_and(bottom, p >= STRAIGHT))(lambda: relay_west(p).start())
        pl.when(jnp.logical_or(east_direct, jnp.logical_and(top, straight)))(
            lambda: send_east(p).start()
        )
        pl.when(jnp.logical_or(west_direct, jnp.logical_and(bottom, straight)))(
            lambda: send_west(p).start()
        )

    def forward(step):
        p = step + STRAIGHT
        pl.when(jnp.logical_and(via, p + AHEAD < count))(lambda: issue(p + AHEAD))

        @pl.when(jnp.logical_and(top, p < count))
        def _():
            relay_east(p).wait_recv()
            onward_east(p).start()

        @pl.when(jnp.logical_and(bottom, p < count))
        def _():
            relay_west(p).wait_recv()
            onward_west(p).start()

    pl.loop(0, READY)(lambda step: issue(READY - 1 - step))

    @pl.loop(READY, count)
    def _(p):
        pack(p)
        pl.when(jnp.logical_not(via))(lambda: issue(p))

        @pl.when(p == READY + 1)
        def _():
            forward(0)

    forward(1)

    own_faces = [courant_ref[pl.ds(layers * f + param, 1), :] for f in range(4)]
    own_factors = face_factors(own_faces, lane_one, has_west, has_east)
    pl.when(has_left)(conc_copies[0].wait_recv)
    pl.when(has_right)(conc_copies[1].wait_recv)
    east = conc_east_in[...].astype(jnp.float32)
    west = conc_west_in[...].astype(jnp.float32)
    conc_halo = jnp.concatenate(
        [jnp.where(first, east, west), rolled(jnp.where(first, west, east), NY)], axis=0
    )
    conc_adv = inner(conc, own_factors) + own_factors[4] * conc_halo
    own_tanh = jnp.tanh(conc_adv)
    own_damping = 1.0 - own_tanh * own_tanh
    wire[param] = own_damping.astype(WIRE)
    damp_copies[0].start()
    damp_copies[1].start()

    forward(2)

    coupling = coupling_ref[...]
    profile = profile_ref[...].T
    own_rates = rates_ref[pl.ds(param, species, stride=layers), :]

    for k in range(profile.shape[1]):
        spread[k] = jnp.broadcast_to(profile[:, k : k + 1], (species, LANES))

    forwarded = [3]

    def forward_next():
        forward(forwarded[0])
        forwarded[0] += 1

    def couple(x):
        top = x.astype(jnp.bfloat16)
        rest = (x - top.astype(jnp.float32)).astype(jnp.bfloat16)
        both = jnp.dot(
            coupling,
            jnp.concatenate([top, rest], axis=1),
            preferred_element_type=jnp.float32,
        )
        return both[:, :LANES] + both[:, LANES:]

    emission = jnp.zeros((species, LANES), jnp.float32)
    for k in range(profile.shape[1]):
        emission += spread[k] * field_ref[pl.ds(layers * k + param, 1), :]

    forward_next()
    damp_copies[0].wait_recv()
    damp_copies[2].start()

    own_dw = section_gamma * own_rates
    own_scaled = own_dw * own_damping

    def solve(right_side):
        scaled = own_damping * right_side
        z = scaled
        for _ in range(ITERS - 1):
            z = scaled + own_scaled * couple(z)
        return right_side + own_dw * couple(z)

    one = solve(emission + own_rates * couple(own_tanh))
    forward_next()
    two = solve(emission + own_rates * couple(jnp.tanh(conc_adv + one)) - 2.0 * one)
    forward_next()
    state_ref[...] = conc_adv + 1.5 * one + 0.5 * two

    for copy in damp_copies[1:]:
        copy.wait_recv()
    for layer in range(layers):
        rate = rates_ref[pl.ds(layer, species, stride=layers), :]
        here = wire[layer].astype(jnp.float32)
        damping[layer] = here
        rates[layer] = rate
        product = rate * here
        for k in range(1, 2 * ITERS + 1):
            factors_dw[k, layer] = (COEFFS[k + 1] / COEFFS[k]) * product
        factors_dw[0, layer] = (COEFFS[1] / COEFFS[0]) * rate

    def lanes(parts):
        return jnp.concatenate(parts, axis=1)

    def gather_edges(p, slot):
        pl.when(has_left)(send_east(p).wait_recv)
        pl.when(has_right)(send_west(p).wait_recv)

        east, west = east_in[p].astype(jnp.float32), west_in[p].astype(jnp.float32)
        here = work.at[slot]
        here[:half] = adv[p, :half] + wide[4][:half] * jnp.where(select, east, west)
        here[half:] = adv[p, half:] + wide[4][half:] * rolled(jnp.where(select, west, east), NY)
        source_index = map_ref[p]
        chosen = spread[source_index]
        field = weight_ref[p] * field_ref[pl.ds(layers * source_index, layers), :]
        a = lanes([here[pl.ds(layer, species, stride=layers), :] for layer in range(layers)])
        source = lanes([chosen * field[layer : layer + 1] for layer in range(layers)])
        return a, source

    def product(z):
        return jnp.dot(coupling, z.astype(jnp.bfloat16), preferred_element_type=jnp.float32)

    @pl.loop(0, count // GROUP)
    def _(group):
        base = group * GROUP
        members = range(GROUP)
        late = count // (2 * GROUP)
        following = forwarded[0] + group + jnp.maximum(group - late, 0)
        forward(following)
        pl.when(group >= late)(lambda: forward(following + 1))

        both = [gather_edges(base + g, g) for g in members]
        d = lanes([damping[layer] for layer in range(layers)])
        w = lanes([rates[layer] for layer in range(layers)])
        v = [w * product(d * a) + source for a, source in both]
        u = [d * value for value in v]
        z = u
        for k in range(2 * ITERS, 0, -1):
            factor = lanes([factors_dw[k, layer] for layer in range(layers)])
            z = [u[g] + factor * product(z[g]) for g in members]
        factor = lanes([factors_dw[0, layer] for layer in range(layers)])
        for g in members:
            out = both[g][0] + v[g] + factor * product(z[g])
            here = work.at[g]
            for layer in range(layers):
                here[pl.ds(layer, species, stride=layers), :] = out[
                    :, layer * LANES : (layer + 1) * LANES
                ]
            result[base + g] = here[...].astype(jnp.bfloat16)
            store(base + g).start()

    for copy in damp_copies:
        copy.wait_send()
    pl.when(has_right)(conc_copies[0].wait_send)
    pl.when(has_left)(conc_copies[1].wait_send)

    @pl.loop(0, count)
    def _(p):
        pl.when(has_right)(send_east(p).wait_send)
        pl.when(has_left)(send_west(p).wait_send)
        pl.when(jnp.logical_and(via, p >= STRAIGHT))(lambda: relay_east(p).wait_send())
        store(p).wait()


def hand_over(state_from, next_from, state_to, next_to, state_held, held, load_sem, store_sem):
    count = next_from.shape[0]

    def pairs(p):
        if p == count:
            return state_from, state_held, state_to
        return next_from.at[p], held.at[p], next_to.at[p]

    def load(p):
        source, here, _ = pairs(p)
        return pltpu.make_async_copy(source, here, load_sem.at[p])

    def store(p):
        _, here, target = pairs(p)
        return pltpu.make_async_copy(here, target, store_sem.at[p])

    for p in range(count + 1):
        load(p).start()
    for p in range(count + 1):
        load(p).wait()
        store(p).start()
    for p in range(count + 1):
        store(p).wait()


def shards(
    concentration,
    reaction_rates,
    coupling,
    profile,
    source_field,
    source_map,
    param_weight,
    sensitivity,
    courant,
):
    tiles, params = lax.axis_size("tile"), lax.axis_size("param")
    species = concentration.shape[0]
    layers = reaction_rates.shape[1]
    count = sensitivity.shape[0]
    sources = profile.shape[0]
    rows = species * layers
    f32, bf16 = jnp.float32, jnp.bfloat16
    vmem = pl.BlockSpec(memory_space=pltpu.VMEM)
    smem = pl.BlockSpec(memory_space=pltpu.SMEM)
    anywhere = pl.BlockSpec(memory_space=pl.ANY)
    halo = pltpu.VMEM((count, rows // 2, LANES), bf16)
    conc_halo = pltpu.VMEM((species // 2, LANES), bf16)
    dma = pltpu.SemaphoreType.DMA
    state, following = pl.pallas_call(
        partial(kernel, tiles, params),
        out_shape=(
            jax.ShapeDtypeStruct((species, LANES), f32),
            jax.ShapeDtypeStruct((count, rows, LANES), bf16),
        ),
        in_specs=[vmem] * 6 + [smem] * 2 + [anywhere],
        out_specs=(vmem, anywhere),
        scratch_shapes=[
            pltpu.VMEM((count, rows, LANES), bf16),
            pltpu.VMEM((count, rows, LANES), f32),
            halo,
            halo,
            halo,
            halo,
            halo,
            conc_halo,
            conc_halo,
            conc_halo,
            conc_halo,
            pltpu.VMEM((layers, species, LANES), f32),
            pltpu.VMEM((layers, species, LANES), WIRE),
            pltpu.VMEM((layers, species, LANES), f32),
            pltpu.VMEM((2 * ITERS + 1, layers, species, LANES), f32),
            pltpu.VMEM((sources, species, LANES), f32),
            pltpu.VMEM((GROUP, rows, LANES), f32),
            pltpu.VMEM((count, rows, LANES), bf16),
            dma((count,)),
            dma((count,)),
            dma((count,)),
            dma((count,)),
            dma((count,)),
            dma((count,)),
            dma((2,)),
            dma((2,)),
            dma((3,)),
            dma((3,)),
            dma((count,)),
            dma((count,)),
        ],
        compiler_params=pltpu.CompilerParams(
            collective_id=0, has_side_effects=True, vmem_limit_bytes=60 << 20
        ),
    )(
        concentration.reshape(species, LANES),
        reaction_rates.reshape(rows, LANES),
        coupling,
        profile,
        source_field.reshape(sources * layers, LANES),
        courant.reshape(4 * layers, LANES),
        source_map,
        param_weight,
        sensitivity.reshape(count, rows, LANES),
    )
    state, following = pl.pallas_call(
        hand_over,
        out_shape=(
            jax.ShapeDtypeStruct((species, LANES), f32),
            jax.ShapeDtypeStruct((count, rows, LANES), bf16),
        ),
        in_specs=[anywhere] * 2,
        out_specs=(anywhere,) * 2,
        scratch_shapes=[
            pltpu.VMEM((species, LANES), f32),
            pltpu.VMEM((count, rows, LANES), bf16),
            dma((count + 1,)),
            dma((count + 1,)),
        ],
        compiler_params=pltpu.CompilerParams(vmem_limit_bytes=60 << 20),
    )(state, following)
    return state.reshape(concentration.shape), following.reshape(sensitivity.shape)


def solution(mesh):
    placed = (
        P(None, "param", "tile"),
        P(None, None, "tile"),
        P(),
        P(),
        P(None, None, "tile"),
        P("param"),
        P("param"),
        P("param", None, None, "tile"),
        P(None, None, "tile"),
    )
    return jax.shard_map(
        shards,
        mesh=mesh,
        in_specs=placed,
        out_specs=(P(None, "param", "tile"), P("param", None, None, "tile")),
        check_vma=False,
    )
```

```python
import math
from functools import partial

import jax
import jax.numpy as jnp
from jax import lax
from jax.experimental import pallas as pl
from jax.experimental.pallas import tpu as pltpu
from jax.sharding import PartitionSpec as P

ITERS = 3
NY = 64
LANES = 128
STRAIGHT = 2
AHEAD = 2
READY = STRAIGHT + AHEAD
DEPTH = 8
WIRE = jnp.bfloat16
GROUP = 2
MESH = pl.DeviceIdType.MESH

section_gamma = 1.0 + 1.0 / math.sqrt(2.0)


def series():
    q = [section_gamma**k for k in range(ITERS + 1)]
    square = [0.0] * (2 * ITERS + 2)
    for i, left in enumerate(q):
        for j, right in enumerate(q):
            square[i + j] += left * right
    c = [-value for value in square]
    for k, value in enumerate(q):
        c[k] += 2.0 * value
    for k in range(2 * ITERS + 1):
        c[k + 1] += 0.5 * square[k]
    return c


COEFFS = series()


def rolled(x, shift):
    return pltpu.roll(x, shift, 1)


def face_factors(rows, lane, has_west, has_east):
    west, east, south, north = rows
    column = lane % NY
    first = lane < NY
    plus = [jnp.maximum(face, 0.0) for face in rows]
    minus = [jnp.minimum(face, 0.0) for face in rows]
    own = 1.0 + minus[0] - plus[1] + minus[2] - plus[3]
    from_south = jnp.where(column == 0, 0.0, plus[2])
    from_north = jnp.where(column == NY - 1, 0.0, -minus[3])
    across = jnp.where(first, -minus[1], plus[0])
    halo = jnp.where(first, plus[0] * has_west, -minus[1] * has_east)
    return own, from_south, from_north, across, halo


def inner(q, factors):
    own, from_south, from_north, across, _ = factors
    return (
        own * q
        + from_south * rolled(q, 1)
        + from_north * rolled(q, LANES - 1)
        + across * rolled(q, NY)
    )


def kernel(
    tiles,
    params,
    conc_ref,
    rates_ref,
    coupling_ref,
    profile_ref,
    field_ref,
    courant_ref,
    map_ref,
    weight_ref,
    sens_ref,
    state_ref,
    next_ref,
    sens,
    adv,
    east_out,
    west_out,
    east_in,
    west_in,
    relay,
    conc_east_out,
    conc_west_out,
    conc_east_in,
    conc_west_in,
    damping,
    wire,
    rates,
    factors_dw,
    spread,
    work,
    result,
    load_sem,
    store_sem,
    east_send,
    east_recv,
    west_send,
    west_recv,
    conc_send,
    conc_recv,
    damp_send,
    damp_recv,
    relay_send,
    relay_recv,
):
    count, rows, _ = sens.shape
    species, layers = coupling_ref.shape[0], params
    half = rows // 2
    param = lax.axis_index("param")
    tile = lax.axis_index("tile")
    right = lax.rem(tile + 1, tiles)
    left = lax.rem(tile + tiles - 1, tiles)
    has_west = (tile > 0).astype(jnp.float32)
    has_east = (tile < tiles - 1).astype(jnp.float32)
    sibling = param + 1 - 2 * lax.rem(param, 2)
    across = lax.rem(param + 2, params)
    peers = [(sibling, tile), (across, tile)]

    def load(p):
        return pltpu.make_async_copy(sens_ref.at[p], sens.at[p], load_sem.at[p])

    def store(p):
        return pltpu.make_async_copy(result.at[p], next_ref.at[p], store_sem.at[p])

    def remote(src, dst, send, recv, device):
        return pltpu.make_async_remote_copy(
            src_ref=src,
            dst_ref=dst,
            send_sem=send,
            recv_sem=recv,
            device_id=device,
            device_id_type=MESH,
        )

    def send_east(p):
        return remote(
            east_out.at[p], east_in.at[p], east_send.at[p], east_recv.at[p], (param, right)
        )

    def send_west(p):
        return remote(
            west_out.at[p], west_in.at[p], west_send.at[p], west_recv.at[p], (param, left)
        )

    conc_copies = [
        remote(conc_east_out, conc_east_in, conc_send.at[0], conc_recv.at[0], (param, right)),
        remote(conc_west_out, conc_west_in, conc_send.at[1], conc_recv.at[1], (param, left)),
    ]
    damp_copies = [
        remote(wire.at[slot], wire.at[slot], damp_send.at[k], damp_recv.at[k], device)
        for k, (slot, device) in enumerate(
            [(param, (across, tile)), (param, (sibling, tile)), (across, (sibling, tile))]
        )
    ]
    has_left, has_right = tile > 0, tile < tiles - 1
    level = lax.rem(tile, DEPTH)
    top = jnp.logical_and(level == DEPTH - 1, has_right)
    bottom = jnp.logical_and(level == 0, has_left)
    via = jnp.logical_or(top, bottom)
    east_direct = jnp.logical_and(level < DEPTH - 1, has_right)
    west_direct = jnp.logical_and(level > 0, has_left)

    def relay_east(p):
        return remote(
            east_out.at[p], relay.at[p], relay_send.at[p], relay_recv.at[p], (across, tile)
        )

    def relay_west(p):
        return remote(
            west_out.at[p], relay.at[p], relay_send.at[p], relay_recv.at[p], (across, tile)
        )

    def onward_east(p):
        return remote(
            relay.at[p], east_in.at[p], east_send.at[p], east_recv.at[p], (across, right)
        )

    def onward_west(p):
        return remote(
            relay.at[p], west_in.at[p], west_send.at[p], west_recv.at[p], (across, left)
        )

    barrier = pltpu.get_barrier_semaphore()
    for device in peers:
        pl.semaphore_signal(barrier, inc=1, device_id=device, device_id_type=MESH)

    @pl.when(has_right)
    def _():
        pl.semaphore_signal(barrier, inc=1, device_id=(param, right), device_id_type=MESH)

    @pl.when(has_left)
    def _():
        pl.semaphore_signal(barrier, inc=1, device_id=(param, left), device_id_type=MESH)

    @pl.when(top)
    def _():
        pl.semaphore_signal(barrier, inc=1, device_id=(across, right), device_id_type=MESH)

    @pl.when(bottom)
    def _():
        pl.semaphore_signal(barrier, inc=1, device_id=(across, left), device_id_type=MESH)

    @pl.when(jnp.logical_not(has_left))
    def _():
        conc_east_in[...] = jnp.zeros_like(conc_east_in)
        east_in[...] = jnp.zeros_like(east_in)

    @pl.when(jnp.logical_not(has_right))
    def _():
        conc_west_in[...] = jnp.zeros_like(conc_west_in)
        west_in[...] = jnp.zeros_like(west_in)

    @pl.loop(0, count)
    def _(p):
        load(p).start()

    lane_wide = lax.broadcasted_iota(jnp.int32, (8, LANES), 1)
    lane_one = lax.broadcasted_iota(jnp.int32, (1, LANES), 1)

    def first_lanes(n):
        return lax.broadcasted_iota(jnp.int32, (n, LANES), 1) < NY

    conc = conc_ref[...]
    low, high = conc[: species // 2], conc[species // 2 :]
    turned = rolled(low, NY)
    first = first_lanes(species // 2)
    conc_east_out[...] = jnp.where(first, turned, high).astype(jnp.bfloat16)
    conc_west_out[...] = jnp.where(first, high, turned).astype(jnp.bfloat16)

    faces = [
        jnp.concatenate([courant_ref[pl.ds(layers * f, layers), :]] * (8 // layers), axis=0)
        for f in range(4)
    ]
    wide = face_factors(faces, lane_wide, has_west, has_east)
    wide = [jnp.tile(factor, (rows // 8, 1)) for factor in wide]
    select = first_lanes(half)

    def pack(p):
        load(p).wait()
        q = sens[p].astype(jnp.float32)
        q_low, q_high = q[:half], q[half:]
        across_low = rolled(q_low, NY)
        east_out[p] = jnp.where(select, across_low, q_high).astype(jnp.bfloat16)
        west_out[p] = jnp.where(select, q_high, across_low).astype(jnp.bfloat16)
        adv[p] = inner(q, wide)

    pl.loop(0, READY)(pack)

    greeted = sum(flag.astype(jnp.int32) for flag in (has_left, has_right, top, bottom))
    pl.semaphore_wait(barrier, len(peers) + greeted)

    pl.when(has_right)(conc_copies[0].start)
    pl.when(has_left)(conc_copies[1].start)

    def issue(p):
        straight = p < STRAIGHT
        pl.when(jnp.logical_and(top, p >= STRAIGHT))(lambda: relay_east(p).start())
        pl.when(jnp.logical_and(bottom, p >= STRAIGHT))(lambda: relay_west(p).start())
        pl.when(jnp.logical_or(east_direct, jnp.logical_and(top, straight)))(
            lambda: send_east(p).start()
        )
        pl.when(jnp.logical_or(west_direct, jnp.logical_and(bottom, straight)))(
            lambda: send_west(p).start()
        )

    def forward(step):
        p = step + STRAIGHT
        pl.when(jnp.logical_and(via, p + AHEAD < count))(lambda: issue(p + AHEAD))

        @pl.when(jnp.logical_and(top, p < count))
        def _():
            relay_east(p).wait_recv()
            onward_east(p).start()

        @pl.when(jnp.logical_and(bottom, p < count))
        def _():
            relay_west(p).wait_recv()
            onward_west(p).start()

    pl.loop(0, READY)(lambda step: issue(READY - 1 - step))

    @pl.loop(READY, count)
    def _(p):
        pack(p)
        pl.when(jnp.logical_not(via))(lambda: issue(p))

        @pl.when(p == count - 4)
        def _():
            forward(0)

    forward(1)

    own_faces = [courant_ref[pl.ds(layers * f + param, 1), :] for f in range(4)]
    own_factors = face_factors(own_faces, lane_one, has_west, has_east)
    pl.when(has_left)(conc_copies[0].wait_recv)
    pl.when(has_right)(conc_copies[1].wait_recv)
    east = conc_east_in[...].astype(jnp.float32)
    west = conc_west_in[...].astype(jnp.float32)
    conc_halo = jnp.concatenate(
        [jnp.where(first, east, west), rolled(jnp.where(first, west, east), NY)], axis=0
    )
    conc_adv = inner(conc, own_factors) + own_factors[4] * conc_halo
    own_tanh = jnp.tanh(conc_adv)
    own_damping = 1.0 - own_tanh * own_tanh
    wire[param] = own_damping.astype(WIRE)
    damp_copies[0].start()
    damp_copies[1].start()

    forward(2)

    coupling = coupling_ref[...]
    profile = profile_ref[...].T
    own_rates = rates_ref[pl.ds(param, species, stride=layers), :]

    for k in range(profile.shape[1]):
        spread[k] = jnp.broadcast_to(profile[:, k : k + 1], (species, LANES))

    forwarded = [3]

    def forward_next():
        forward(forwarded[0])
        forwarded[0] += 1

    def couple(x):
        top = x.astype(jnp.bfloat16)
        rest = (x - top.astype(jnp.float32)).astype(jnp.bfloat16)
        both = jnp.dot(
            coupling,
            jnp.concatenate([top, rest], axis=1),
            preferred_element_type=jnp.float32,
        )
        return both[:, :LANES] + both[:, LANES:]

    emission = jnp.zeros((species, LANES), jnp.float32)
    for k in range(profile.shape[1]):
        emission += spread[k] * field_ref[pl.ds(layers * k + param, 1), :]

    forward_next()
    damp_copies[0].wait_recv()
    damp_copies[2].start()

    own_dw = section_gamma * own_rates
    own_scaled = own_dw * own_damping

    def solve(right_side):
        scaled = own_damping * right_side
        z = scaled
        for _ in range(ITERS - 1):
            z = scaled + own_scaled * couple(z)
        return right_side + own_dw * couple(z)

    one = solve(emission + own_rates * couple(own_tanh))
    forward_next()
    two = solve(emission + own_rates * couple(jnp.tanh(conc_adv + one)) - 2.0 * one)
    forward_next()
    state_ref[...] = conc_adv + 1.5 * one + 0.5 * two

    for copy in damp_copies[1:]:
        copy.wait_recv()
    for layer in range(layers):
        rate = rates_ref[pl.ds(layer, species, stride=layers), :]
        here = wire[layer].astype(jnp.float32)
        damping[layer] = here
        rates[layer] = rate
        product = rate * here
        for k in range(1, 2 * ITERS + 1):
            factors_dw[k, layer] = (COEFFS[k + 1] / COEFFS[k]) * product
        factors_dw[0, layer] = (COEFFS[1] / COEFFS[0]) * rate

    def lanes(parts):
        return jnp.concatenate(parts, axis=1)

    def gather_edges(p, slot):
        pl.when(has_left)(send_east(p).wait_recv)
        pl.when(has_right)(send_west(p).wait_recv)

        east, west = east_in[p].astype(jnp.float32), west_in[p].astype(jnp.float32)
        here = work.at[slot]
        here[:half] = adv[p, :half] + wide[4][:half] * jnp.where(select, east, west)
        here[half:] = adv[p, half:] + wide[4][half:] * rolled(jnp.where(select, west, east), NY)
        source_index = map_ref[p]
        chosen = spread[source_index]
        field = weight_ref[p] * field_ref[pl.ds(layers * source_index, layers), :]
        a = lanes([here[pl.ds(layer, species, stride=layers), :] for layer in range(layers)])
        source = lanes([chosen * field[layer : layer + 1] for layer in range(layers)])
        return a, source

    def product(z):
        return jnp.dot(coupling, z.astype(jnp.bfloat16), preferred_element_type=jnp.float32)

    @pl.loop(0, count // GROUP)
    def _(group):
        base = group * GROUP
        members = range(GROUP)
        late = count // (2 * GROUP)
        following = forwarded[0] + group + jnp.maximum(group - late, 0)
        forward(following)
        pl.when(group >= late)(lambda: forward(following + 1))

        both = [gather_edges(base + g, g) for g in members]
        d = lanes([damping[layer] for layer in range(layers)])
        w = lanes([rates[layer] for layer in range(layers)])
        v = [w * product(d * a) + source for a, source in both]
        u = [d * value for value in v]
        z = u
        for k in range(2 * ITERS, 0, -1):
            factor = lanes([factors_dw[k, layer] for layer in range(layers)])
            z = [u[g] + factor * product(z[g]) for g in members]
        factor = lanes([factors_dw[0, layer] for layer in range(layers)])
        for g in members:
            out = both[g][0] + v[g] + factor * product(z[g])
            here = work.at[g]
            for layer in range(layers):
                here[pl.ds(layer, species, stride=layers), :] = out[
                    :, layer * LANES : (layer + 1) * LANES
                ]
            result[base + g] = here[...].astype(jnp.bfloat16)
            store(base + g).start()

    for copy in damp_copies:
        copy.wait_send()
    pl.when(has_right)(conc_copies[0].wait_send)
    pl.when(has_left)(conc_copies[1].wait_send)

    @pl.loop(0, count)
    def _(p):
        pl.when(has_right)(send_east(p).wait_send)
        pl.when(has_left)(send_west(p).wait_send)
        pl.when(jnp.logical_and(via, p >= STRAIGHT))(lambda: relay_east(p).wait_send())
        store(p).wait()


def hand_over(state_from, next_from, state_to, next_to, state_held, held, load_sem, store_sem):
    count = next_from.shape[0]

    def pairs(p):
        if p == count:
            return state_from, state_held, state_to
        return next_from.at[p], held.at[p], next_to.at[p]

    def load(p):
        source, here, _ = pairs(p)
        return pltpu.make_async_copy(source, here, load_sem.at[p])

    def store(p):
        _, here, target = pairs(p)
        return pltpu.make_async_copy(here, target, store_sem.at[p])

    for p in range(count + 1):
        load(p).start()
    for p in range(count + 1):
        load(p).wait()
        store(p).start()
    for p in range(count + 1):
        store(p).wait()


def shards(
    concentration,
    reaction_rates,
    coupling,
    profile,
    source_field,
    source_map,
    param_weight,
    sensitivity,
    courant,
):
    tiles, params = lax.axis_size("tile"), lax.axis_size("param")
    species = concentration.shape[0]
    layers = reaction_rates.shape[1]
    count = sensitivity.shape[0]
    sources = profile.shape[0]
    rows = species * layers
    f32, bf16 = jnp.float32, jnp.bfloat16
    vmem = pl.BlockSpec(memory_space=pltpu.VMEM)
    smem = pl.BlockSpec(memory_space=pltpu.SMEM)
    anywhere = pl.BlockSpec(memory_space=pl.ANY)
    halo = pltpu.VMEM((count, rows // 2, LANES), bf16)
    conc_halo = pltpu.VMEM((species // 2, LANES), bf16)
    dma = pltpu.SemaphoreType.DMA
    state, following = pl.pallas_call(
        partial(kernel, tiles, params),
        out_shape=(
            jax.ShapeDtypeStruct((species, LANES), f32),
            jax.ShapeDtypeStruct((count, rows, LANES), bf16),
        ),
        in_specs=[vmem] * 6 + [smem] * 2 + [anywhere],
        out_specs=(vmem, anywhere),
        scratch_shapes=[
            pltpu.VMEM((count, rows, LANES), bf16),
            pltpu.VMEM((count, rows, LANES), f32),
            halo,
            halo,
            halo,
            halo,
            halo,
            conc_halo,
            conc_halo,
            conc_halo,
            conc_halo,
            pltpu.VMEM((layers, species, LANES), f32),
            pltpu.VMEM((layers, species, LANES), WIRE),
            pltpu.VMEM((layers, species, LANES), f32),
            pltpu.VMEM((2 * ITERS + 1, layers, species, LANES), f32),
            pltpu.VMEM((sources, species, LANES), f32),
            pltpu.VMEM((GROUP, rows, LANES), f32),
            pltpu.VMEM((count, rows, LANES), bf16),
            dma((count,)),
            dma((count,)),
            dma((count,)),
            dma((count,)),
            dma((count,)),
            dma((count,)),
            dma((2,)),
            dma((2,)),
            dma((3,)),
            dma((3,)),
            dma((count,)),
            dma((count,)),
        ],
        compiler_params=pltpu.CompilerParams(
            collective_id=0, has_side_effects=True, vmem_limit_bytes=60 << 20
        ),
    )(
        concentration.reshape(species, LANES),
        reaction_rates.reshape(rows, LANES),
        coupling,
        profile,
        source_field.reshape(sources * layers, LANES),
        courant.reshape(4 * layers, LANES),
        source_map,
        param_weight,
        sensitivity.reshape(count, rows, LANES),
    )
    state, following = pl.pallas_call(
        hand_over,
        out_shape=(
            jax.ShapeDtypeStruct((species, LANES), f32),
            jax.ShapeDtypeStruct((count, rows, LANES), bf16),
        ),
        in_specs=[anywhere] * 2,
        out_specs=(anywhere,) * 2,
        scratch_shapes=[
            pltpu.VMEM((species, LANES), f32),
            pltpu.VMEM((count, rows, LANES), bf16),
            dma((count + 1,)),
            dma((count + 1,)),
        ],
        compiler_params=pltpu.CompilerParams(vmem_limit_bytes=60 << 20),
    )(state, following)
    return state.reshape(concentration.shape), following.reshape(sensitivity.shape)


def solution(mesh):
    placed = (
        P(None, "param", "tile"),
        P(None, None, "tile"),
        P(),
        P(),
        P(None, None, "tile"),
        P("param"),
        P("param"),
        P("param", None, None, "tile"),
        P(None, None, "tile"),
    )
    return jax.shard_map(
        shards,
        mesh=mesh,
        in_specs=placed,
        out_specs=(P(None, "param", "tile"), P("param", None, None, "tile")),
        check_vma=False,
    )
```
